32 devices in a mesh: leaf: 2 (over y), row: 4 (over z), col: 4 (over x, core).
Axes of the slice: x: 2, y: 2, z: 4, core: 2. Of those that a mesh axis runs over, the one named last changes fastest.
Arguments:
- child_front: float32 [2, 4096, 4096], P('leaf', 'row', 'col'), may hold values from -2 to 4, as said below
- parent_front: float32 [8192, 8, 8, 128], P('row', None, ('leaf', 'col')), may hold values from -2 to 4, as said below
- block_map: int32 [2, 30], replicated, may hold values from 0 to 63, as said below
Outputs:
- child_factor: float32 [2, 4096, 256], P('leaf', 'row')
- parent_out: float32 [8192, 8, 8, 128], P('row', None, ('leaf', 'col'))
The draws below stay inside these ranges and needn't reach their ends.
Inputs may be any that keep to these rules, and one draw needn't show every extreme that they name: `child_front`: each child front is symmetric positive definite, with smallest eigenvalue above 0.1. `parent_front`: viewed as a 8192 x 8192 matrix, the parent front is symmetric positive definite, with smallest eigenvalue above 0.1. `block_map`: row c lists, in order, the parent block that receives each of the 30 trailing blocks of child front c; the entries of a row are distinct parent blocks. Put 2 empty blocks in front of a row and cut it into aligned groups of 8: in every group at most 2 entries share the value of entry // 16, and at most 2 share the value of entry modulo 4; both bounds are reached.
All inputs are finite; a program needn't handle non-finite values.
Results may differ from the reference program's by a relative error of at most 0.0001.
Values sent between devices are 32-bit elements; how exact they have to be, the bound alone decides.
A program may use at most 128 MiB of HBM per device.

```python
import jax
import jax.numpy as jnp
from jax import lax

FC = 4096
FP = 8192
PANEL = 256
BLOCK = 128
CHILDREN = 2
GRID = 4
NB_C = 32
MB = 30
CB = 8
PR = 16
NCD = 8
KB = 8
SPREAD = 4


def symmetric_front(key, order):
    inner_width = max(order // 8, 64)
    factor_key, lift_key, noise_key = jax.random.split(key, 3)
    factor = jax.random.normal(factor_key, (order, inner_width), jnp.float32)
    diagonal = jax.random.uniform(lift_key, (order,), jnp.float32, 0.25, 0.65)
    noise = jax.random.normal(noise_key, (order, order), jnp.float32)
    coupled = jnp.dot(factor, factor.T, precision=lax.Precision.HIGHEST, preferred_element_type=jnp.float32) / inner_width
    coupled = 0.5 * (coupled + coupled.T)
    rough_part = (noise + noise.T) * (0.03 / jnp.sqrt(2.0 * order))
    return coupled + rough_part + jnp.diag(diagonal)


def draw_child_front(key, part):
    base = jax.random.fold_in(key, 11)
    fronts = [symmetric_front(jax.random.fold_in(base, child), FC) for child in range(CHILDREN)]
    return jnp.stack(fronts)


def draw_parent_front(key, part):
    whole_front = symmetric_front(jax.random.fold_in(key, 101), FP)
    return whole_front.reshape(FP, KB, NCD, BLOCK)


def draw_block_map(key, part):
    base = jax.random.fold_in(key, 202)
    listing = []
    for child in range(CHILDREN):
        child_key = jax.random.fold_in(base, child)
        key_row, key_col, key_extra, key_slot = jax.random.split(child_key, 4)
        perm_row = jax.random.permutation(key_row, GRID)
        perm_col = jax.random.permutation(key_col, GRID)
        perm_extra = jax.random.permutation(key_extra, SPREAD)
        slot_keys = jax.random.split(key_slot, GRID)
        slot_perm = jax.vmap(lambda one_key: jax.random.permutation(one_key, CB))(slot_keys)
        position = jnp.arange(NB_C, dtype=jnp.int32)
        group = position // CB
        slot = slot_perm[group, position % CB]
        first = (group + slot) % GRID
        second = (2 * group + slot) % GRID
        extra = slot // GRID
        target = perm_row[first] * PR + perm_extra[extra] * GRID + perm_col[second]
        listing.append(target[NB_C - MB:])
    return jnp.stack(listing).astype(jnp.int32)


def setup_inputs(seed: int = 0) -> dict:
    keys = jax.random.split(jax.random.key(seed), 4)
    return {
        "child_front": draw_child_front(jax.random.fold_in(keys[3], 71), 0),
        "parent_front": draw_parent_front(jax.random.fold_in(keys[3], 71), 0),
        "block_map": draw_block_map(jax.random.fold_in(keys[3], 71), 0),
    }


def matmul(left, right):
    return jnp.dot(left.astype(jnp.float32), right.astype(jnp.float32), precision=lax.Precision.HIGHEST, preferred_element_type=jnp.float32)

def factor_panel(front):
    lower_factor = jnp.linalg.cholesky(front[:PANEL, :PANEL])
    identity = jnp.eye(PANEL, dtype=jnp.float32)
    inverse = jax.scipy.linalg.solve_triangular(lower_factor, identity, lower=True)
    panel = matmul(front[:, :PANEL], inverse.T)
    upper = matmul(inverse, front[:PANEL, PANEL:])
    schur = front[PANEL:, PANEL:] - matmul(panel[PANEL:], upper)
    return (panel, schur)

def reference(child_front, parent_front, block_map):
    assembled = parent_front.reshape(FP, FP)
    offsets = jnp.arange(BLOCK, dtype=jnp.int32)
    factors = []
    for child in range(CHILDREN):
        panel, contribution = factor_panel(child_front[child])
        factors.append(panel)
        targets = (block_map[child].astype(jnp.int32)[:, None] * BLOCK + offsets[None, :]).reshape(-1)
        assembled = assembled.at[targets[:, None], targets[None, :]].add(contribution)
    panel, schur = factor_panel(assembled)
    result = assembled.at[PANEL:, PANEL:].set(schur).at[:, :PANEL].set(panel)
    return (jnp.stack(factors), result.reshape(FP, KB, NCD, BLOCK))
```

```python
import functools

import jax
import jax.numpy as jnp
from jax import lax
from jax.experimental import pallas as pl
from jax.experimental.pallas import tpu as pltpu
from jax.sharding import PartitionSpec as P

PANEL = 256
BLOCK = 128
STEP = 64
HIGH = lax.Precision.HIGHEST
F32 = jnp.float32


def dot(left, right, dims=((1,), (0,))):
    return lax.dot_general(left, right, (dims, ((), ())), precision=HIGH, preferred_element_type=F32)


def spread(x, axis, unit):
    n = lax.axis_size(axis)
    here = lax.axis_index(axis)
    stride = n // 2
    while stride >= unit:
        pairs = [
            (i + e, i + stride + e) for i in range(0, n, 2 * stride) for e in range(unit)
        ]
        got = lax.ppermute(x, axis, pairs)
        inside = here % (2 * stride)
        x = jnp.where((inside >= stride) & (inside < stride + unit), got, x)
        stride //= 2
    return x


def swap_pairs(x):
    n = lax.axis_size("col")
    here = lax.axis_index("col")
    got = lax.ppermute(x, "col", [(i, i ^ 1) for i in range(n)])
    even = here % 2 == 0
    return jnp.where(even, x, got), jnp.where(even, got, x)


def invert_kernel(left_ref, right_ref, out_ref, work):
    work[:, 0:BLOCK] = left_ref[...]
    work[:, BLOCK:PANEL] = right_ref[...]
    rows = lax.broadcasted_iota(jnp.int32, (PANEL, PANEL), 0)
    cols = lax.broadcasted_iota(jnp.int32, (PANEL, PANEL), 1)
    work[:, PANEL:] = (rows == cols).astype(F32)
    groups = STEP // 8
    sub = lax.broadcasted_iota(jnp.int32, (8, 1), 0)
    lane8 = lax.broadcasted_iota(jnp.int32, (8, BLOCK), 1)
    sub8 = lax.broadcasted_iota(jnp.int32, (8, BLOCK), 0)
    for s in range(PANEL // STEP):
        top = s * STEP
        tile = top // BLOCK * BLOCK
        off = top - tile
        d = [work[top + 8 * g : top + 8 * g + 8, tile : tile + BLOCK] for g in range(groups)]
        w = [(lane8 == sub8 + 8 * g).astype(F32) for g in range(groups)]
        for j in range(STEP):
            g0 = j // 8
            r = j % 8
            drow = d[g0][r : r + 1, :]
            wrow = w[g0][r : r + 1, :]
            inv = 1.0 / drow[:, off + j : off + j + 1]
            drow = drow * inv
            wrow = wrow * inv
            for g in range(g0, groups):
                f = d[g][:, off + j : off + j + 1]
                if g == g0:
                    if r == 7:
                        continue
                    f = jnp.where(sub > r, f, 0.0)
                d[g] = d[g] - f * drow
                w[g] = w[g] - f * wrow
        scaled = []
        for g in range(groups):
            diag = jnp.sum(jnp.where(lane8 == sub8 + (off + 8 * g), d[g], 0.0), axis=1, keepdims=True)
            scaled.append(w[g] * lax.rsqrt(diag))
        wide = jnp.concatenate(scaled, axis=0)[:, :STEP]
        strip = dot(wide, work[top : top + STEP, :])
        work[top : top + STEP, :] = strip
        if top + STEP < PANEL:
            change = dot(strip[:, :PANEL], strip, ((0,), (0,)))
            work[top + STEP :, :] = work[top + STEP :, :] - change[top + STEP :, :]
    out_ref[...] = work[:, PANEL:]


def lower_inverse(left, right):
    return pl.pallas_call(
        invert_kernel,
        out_shape=jax.ShapeDtypeStruct((PANEL, PANEL), F32),
        scratch_shapes=[pltpu.VMEM((PANEL, 2 * PANEL), F32)],
        cost_estimate=pl.CostEstimate(flops=10**10, bytes_accessed=10**8, transcendentals=0),
        name="invert",
    )(left, right)


def schur_kernel(slots, row_ids, col_ids, a_ref, f_ref, u_ref, out_ref, strip):
    strip[...] = a_ref[...] - dot(f_ref[...], u_ref[...])
    for m in range(slots):
        start = pl.multiple_of(col_ids[m] * BLOCK, BLOCK)
        out_ref[m] = strip[:, pl.ds(start, BLOCK)]


def schur_pick(front, factor, upper, row_ids, col_ids):
    dests, slots = row_ids.shape[0], col_ids.shape[0]
    width = front.shape[1]
    return pl.pallas_call(
        functools.partial(schur_kernel, slots),
        grid_spec=pltpu.PrefetchScalarGridSpec(
            num_scalar_prefetch=2,
            grid=(dests,),
            in_specs=[
                pl.BlockSpec((BLOCK, width), lambda i, r, c: (r[i], 0)),
                pl.BlockSpec((BLOCK, PANEL), lambda i, r, c: (r[i], 0)),
                pl.BlockSpec((PANEL, width), lambda i, r, c: (0, 0)),
            ],
            out_specs=pl.BlockSpec((None, slots, BLOCK, BLOCK), lambda i, r, c: (i, 0, 0, 0)),
            scratch_shapes=[pltpu.VMEM((BLOCK, width), F32)],
        ),
        out_shape=jax.ShapeDtypeStruct((dests, slots, BLOCK, BLOCK), F32),
        cost_estimate=pl.CostEstimate(
            flops=12 * dests * BLOCK * PANEL * width,
            bytes_accessed=8 * dests * BLOCK * width,
            transcendentals=0,
        ),
        name="schur",
    )(row_ids, col_ids, front, factor, upper)


def assemble_kernel(leaves, capacity, kblocks, rfrom, rok, cfrom, cok, parent_ref, *refs):
    out_ref = refs[-1]
    p = pl.program_id(0)
    for k in range(kblocks):
        total = parent_ref[pl.ds(k, BLOCK, stride=kblocks), :]
        for s in range(leaves):
            m = cfrom[s * kblocks + k]
            for t in range(capacity):
                ok = rok[(s * capacity + t) * pl.num_programs(0) + p] * cok[s * kblocks + k]
                total = total + jnp.where(ok > 0, refs[s * capacity + t][m], 0.0)
        out_ref[:, k * BLOCK : (k + 1) * BLOCK] = total


def assemble(parent, pieces, leaves, capacity, kblocks, rfrom, rok, cfrom, cok):
    per_row = parent.shape[0] // (BLOCK * kblocks)
    slots = pieces[0].shape[1]

    def piece_spec(n):
        return pl.BlockSpec(
            (None, slots, BLOCK, BLOCK), lambda i, rf, ro, cf, co: (rf[n * per_row + i], 0, 0, 0)
        )

    return pl.pallas_call(
        functools.partial(assemble_kernel, leaves, capacity, kblocks),
        grid_spec=pltpu.PrefetchScalarGridSpec(
            num_scalar_prefetch=4,
            grid=(per_row,),
            in_specs=[pl.BlockSpec((BLOCK * kblocks, BLOCK), lambda i, *_: (i, 0))]
            + [piece_spec(n) for n in range(len(pieces))],
            out_specs=pl.BlockSpec((BLOCK, kblocks * BLOCK), lambda i, *_: (i, 0)),
        ),
        out_shape=jax.ShapeDtypeStruct((per_row * BLOCK, kblocks * BLOCK), F32),
        compiler_params=pltpu.CompilerParams(vmem_limit_bytes=40 * 2**20),
        name="assemble",
    )(rfrom, rok, cfrom, cok, parent, *pieces)


def update_kernel(kblocks, lead, place, a_ref, p0_ref, p1_ref, inv_ref, top_ref, out_ref, upper):
    p = pl.program_id(0)

    @pl.when(p == 0)
    def _():
        upper[...] = dot(inv_ref[...], top_ref[...])

    factor = dot(p0_ref[...], inv_ref[:, :BLOCK], ((1,), (1,)))
    factor = factor + dot(p1_ref[...], inv_ref[:, BLOCK:], ((1,), (1,)))
    keep = (place[0] == 0) & (p < lead)
    for k in range(kblocks):
        span = slice(k * BLOCK, (k + 1) * BLOCK)
        mine = a_ref[:, span]
        value = jnp.where(keep, mine, mine - dot(factor, upper[:, span]))
        if k == 0:
            for block in range(lead):
                piece = factor[:, block * BLOCK : (block + 1) * BLOCK]
                value = jnp.where(place[1] == block, piece, value)
        out_ref[pl.ds(k, BLOCK, stride=kblocks), :] = value


def update(assembled, panel0, panel1, inverse, top, place, kblocks):
    rows, width = assembled.shape
    return pl.pallas_call(
        functools.partial(update_kernel, kblocks, PANEL // BLOCK),
        grid_spec=pltpu.PrefetchScalarGridSpec(
            num_scalar_prefetch=1,
            grid=(rows // BLOCK,),
            in_specs=[
                pl.BlockSpec((BLOCK, width), lambda i, _: (i, 0)),
                pl.BlockSpec((BLOCK, BLOCK), lambda i, _: (i, 0)),
                pl.BlockSpec((BLOCK, BLOCK), lambda i, _: (i, 0)),
                pl.BlockSpec((PANEL, PANEL), lambda i, _: (0, 0)),
                pl.BlockSpec((PANEL, width), lambda i, _: (0, 0)),
            ],
            out_specs=pl.BlockSpec((BLOCK * kblocks, BLOCK), lambda i, _: (i, 0)),
            scratch_shapes=[pltpu.VMEM((PANEL, width), F32)],
        ),
        out_shape=jax.ShapeDtypeStruct((rows * kblocks, BLOCK), F32),
        name="update",
    )(place, assembled, panel0, panel1, inverse, top)


def ranks(targets, usable):
    count = targets.shape[-1]
    same = (targets[..., :, None] == targets[..., None, :]) & usable[..., None, :]
    before = jnp.arange(count)[None, :] < jnp.arange(count)[:, None]
    return jnp.sum(same & before, axis=-1)


def per_device(child_front, parent_front, block_map):
    front = child_front[0]
    grid_rows = lax.axis_size("row")
    grid_cols = lax.axis_size("col")
    leaves = lax.axis_size("leaf")
    row_id = lax.axis_index("row")
    col_id = lax.axis_index("col")
    leaf_id = lax.axis_index("leaf")
    blocks = front.shape[0] // BLOCK
    capacity = max(1, blocks // grid_rows)
    parent_rows, kblocks = parent_front.shape[:2]
    per_row = parent_rows // BLOCK
    period = leaves * grid_cols
    lead = PANEL // BLOCK

    corner = spread(spread(front[:PANEL, :PANEL], "row", 1), "col", 1)
    corner, panel_rows, top_rows = lax.optimization_barrier(
        (corner, front[:, :PANEL], front[:PANEL, :])
    )
    panel_rows = spread(panel_rows, "col", 1)
    top_rows = spread(top_rows, "row", 1)
    inverse = lower_inverse(corner[:, :BLOCK], corner[:, BLOCK:])

    padded = jnp.concatenate([jnp.full((leaves, lead), -1, jnp.int32), block_map], axis=1)
    maps = padded.reshape(leaves, grid_rows, blocks)
    usable = maps >= 0
    to_row = jnp.where(usable, maps // per_row, -1)
    to_col = jnp.where(usable, maps % grid_cols, -1)
    row_rank = ranks(to_row, usable)
    col_rank = ranks(to_col, usable)
    positions = jnp.arange(blocks)

    def picks(target, rank, group, count):
        target = target[leaf_id, group]
        rank = rank[leaf_id, group]
        chosen = (target == jnp.arange(count)[:, None, None]) & (
            rank == jnp.arange(capacity)[None, :, None]
        )
        return jnp.sum(jnp.where(chosen, positions, 0), axis=-1).astype(jnp.int32)

    row_ids = picks(to_row, row_rank, row_id, grid_rows)
    col_ids = picks(to_col, col_rank, col_id, grid_cols).reshape(-1)

    order = (leaf_id - jnp.arange(leaves)) % leaves
    maps_here = maps[order]
    row_rank_here = row_rank[order]
    col_rank_here = col_rank[order]
    group = jnp.arange(grid_rows)[None, None, :, None]
    hit = maps_here[:, None] == (row_id * per_row + jnp.arange(per_row))[None, :, None, None]
    in_chunk = row_rank_here[:, None, None] == jnp.arange(capacity)[None, :, None, None, None]
    hit_chunk = hit[:, None] & in_chunk
    rfrom = jnp.sum(jnp.where(hit_chunk, group[:, None], 0), axis=(-1, -2))
    rok = jnp.sum(hit_chunk, axis=(-1, -2))
    owned = jnp.arange(kblocks) * period + leaf_id * grid_cols + col_id
    hit = maps_here[:, None] == owned[None, :, None, None]
    slot = group * capacity + col_rank_here[:, None]
    cfrom = jnp.sum(jnp.where(hit, slot, 0), axis=(-1, -2))
    cok = jnp.sum(hit, axis=(-1, -2))
    rfrom, rok, cfrom, cok = [x.reshape(-1).astype(jnp.int32) for x in (rfrom, rok, cfrom, cok)]

    factor = dot(panel_rows, inverse, ((1,), (1,)))
    upper = dot(inverse, top_rows)
    own = []
    for t in range(capacity):
        out = schur_pick(front, factor, upper, row_ids[:, t], col_ids)
        out = out.reshape(grid_rows * grid_cols, capacity, BLOCK, BLOCK)
        got = lax.all_to_all(out, ("row", "col"), split_axis=0, concat_axis=0, tiled=True)
        own.append(got)
    pieces = [[] for _ in range(leaves)]
    for got in own:
        for shift in range(leaves):
            moved = got
            if shift:
                pairs = [(i, (i + shift) % leaves) for i in range(leaves)]
                moved = lax.ppermute(got, "leaf", pairs)
            pieces[shift].append(
                moved.reshape(grid_rows, grid_cols * capacity, BLOCK, BLOCK)
            )
    pieces = [x for part in pieces for x in part]
    assembled = assemble(
        parent_front.reshape(parent_rows * kblocks, BLOCK),
        pieces, leaves, capacity, kblocks, rfrom, rok, cfrom, cok,
    )

    piece = spread(spread(assembled[:PANEL, :BLOCK], "col", 2), "leaf", 1)
    piece, panel = lax.optimization_barrier((piece, assembled[:, :BLOCK]))
    panel = spread(spread(panel, "col", 2), "leaf", 1)
    panel0, panel1 = swap_pairs(panel)
    corner0, corner1 = swap_pairs(spread(piece, "row", 1))
    corner0, corner1, top = lax.optimization_barrier((corner0, corner1, assembled[:PANEL]))
    top = spread(top, "row", 1)
    inverse_parent = lower_inverse(corner0, corner1)
    place = jnp.stack([row_id, leaf_id * grid_cols + col_id]).astype(jnp.int32)
    result = update(assembled, panel0, panel1, inverse_parent, top, place, kblocks)
    return factor[None], result.reshape(parent_front.shape)


def solution(mesh):
    placed = (P("leaf", "row", "col"), P("row", None, ("leaf", "col"), None), P())
    return jax.shard_map(
        per_device,
        mesh=mesh,
        in_specs=placed,
        out_specs=(P("leaf", "row", None), P("row", None, ("leaf", "col"), None)),
        check_vma=False,
    )
```

```python
import functools

import jax
import jax.numpy as jnp
from jax import lax
from jax.experimental import pallas as pl
from jax.experimental.pallas import tpu as pltpu
from jax.sharding import PartitionSpec as P

PANEL = 256
BLOCK = 128
STEP = 64
HIGH = lax.Precision.HIGHEST
F32 = jnp.float32


def dot(left, right, dims=((1,), (0,))):
    return lax.dot_general(left, right, (dims, ((), ())), precision=HIGH, preferred_element_type=F32)


def split(x):
    high = x.astype(jnp.bfloat16)
    return high, (x - high.astype(F32)).astype(jnp.bfloat16)


def dot_split(left, right):
    one = lambda a, b: jnp.dot(a, b, preferred_element_type=F32)
    return one(left[0], right[0]) + (one(left[0], right[1]) + one(left[1], right[0]))


def spread(x, axis, unit):
    n = lax.axis_size(axis)
    here = lax.axis_index(axis)
    stride = n // 2
    while stride >= unit:
        pairs = [
            (i + e, i + stride + e) for i in range(0, n, 2 * stride) for e in range(unit)
        ]
        got = lax.ppermute(x, axis, pairs)
        inside = here % (2 * stride)
        x = jnp.where((inside >= stride) & (inside < stride + unit), got, x)
        stride //= 2
    return x


def swap_pairs(x):
    n = lax.axis_size("col")
    here = lax.axis_index("col")
    got = lax.ppermute(x, "col", [(i, i ^ 1) for i in range(n)])
    even = here % 2 == 0
    return jnp.where(even, x, got), jnp.where(even, got, x)


def invert_kernel(left_ref, right_ref, out_ref, work):
    work[:, 0:BLOCK] = left_ref[...]
    work[:, BLOCK:PANEL] = right_ref[...]
    rows = lax.broadcasted_iota(jnp.int32, (PANEL, PANEL), 0)
    cols = lax.broadcasted_iota(jnp.int32, (PANEL, PANEL), 1)
    work[:, PANEL:] = (rows == cols).astype(F32)
    groups = STEP // 8
    sub = lax.broadcasted_iota(jnp.int32, (8, 1), 0)
    lane8 = lax.broadcasted_iota(jnp.int32, (8, BLOCK), 1)
    sub8 = lax.broadcasted_iota(jnp.int32, (8, BLOCK), 0)
    for s in range(PANEL // STEP):
        top = s * STEP
        tile = top // BLOCK * BLOCK
        off = top - tile
        d = [work[top + 8 * g : top + 8 * g + 8, tile : tile + BLOCK] for g in range(groups)]
        w = [(lane8 == sub8 + 8 * g).astype(F32) for g in range(groups)]
        for j in range(STEP):
            g0 = j // 8
            r = j % 8
            drow = d[g0][r : r + 1, :]
            wrow = w[g0][r : r + 1, :]
            inv = 1.0 / drow[:, off + j : off + j + 1]
            drow = drow * inv
            wrow = wrow * inv
            for g in range(g0, groups):
                f = d[g][:, off + j : off + j + 1]
                if g == g0:
                    if r == 7:
                        continue
                    f = jnp.where(sub > r, f, 0.0)
                d[g] = d[g] - f * drow
                w[g] = w[g] - f * wrow
        scaled = []
        for g in range(groups):
            diag = jnp.sum(jnp.where(lane8 == sub8 + (off + 8 * g), d[g], 0.0), axis=1, keepdims=True)
            scaled.append(w[g] * lax.rsqrt(diag))
        wide = jnp.concatenate(scaled, axis=0)[:, :STEP]
        strip = dot(wide, work[top : top + STEP, :])
        work[top : top + STEP, :] = strip
        if top + STEP < PANEL:
            change = dot(strip[:, :PANEL], strip, ((0,), (0,)))
            work[top + STEP :, :] = work[top + STEP :, :] - change[top + STEP :, :]
    out_ref[...] = work[:, PANEL:]


def lower_inverse(left, right):
    return pl.pallas_call(
        invert_kernel,
        out_shape=jax.ShapeDtypeStruct((PANEL, PANEL), F32),
        scratch_shapes=[pltpu.VMEM((PANEL, 2 * PANEL), F32)],
        cost_estimate=pl.CostEstimate(flops=10**10, bytes_accessed=10**8, transcendentals=0),
        name="invert",
    )(left, right)


def pick_kernel(capacity, row_ids, col_ids, *refs):
    outs = refs[capacity:]
    for t in range(capacity):
        for m in range(col_ids.shape[0]):
            start = pl.multiple_of(col_ids[m] * BLOCK, BLOCK)
            outs[t * capacity + m % capacity][m // capacity] = refs[t][:, pl.ds(start, BLOCK)]


def pick_blocks(front, row_ids, col_ids, capacity):
    dests = row_ids.shape[0] // capacity
    ends = col_ids.shape[0] // capacity
    width = front.shape[1]

    def rows(t):
        return pl.BlockSpec((BLOCK, width), lambda i, r, c: (r[i * capacity + t], 0))

    return pl.pallas_call(
        functools.partial(pick_kernel, capacity),
        grid_spec=pltpu.PrefetchScalarGridSpec(
            num_scalar_prefetch=2,
            grid=(dests,),
            in_specs=[rows(t) for t in range(capacity)],
            out_specs=[
                pl.BlockSpec((None, ends, BLOCK, BLOCK), lambda i, r, c: (i, 0, 0, 0))
            ] * capacity**2,
        ),
        out_shape=[jax.ShapeDtypeStruct((dests, ends, BLOCK, BLOCK), F32)] * capacity**2,
        name="pick",
    )(row_ids, col_ids, *[front] * capacity)


def assemble_kernel(leaves, capacity, kblocks, rfrom, rok, rslot, cfrom, cok, parent_ref, *refs):
    squares = capacity**2
    blocks = refs[: leaves * squares]
    factors = refs[leaves * squares : leaves * (squares + 1)]
    uppers = refs[leaves * (squares + 1) : leaves * (squares + 2)]
    out_ref, high, low = refs[-3:]
    p = pl.program_id(0)
    steps = pl.num_programs(0)

    @pl.when(p == 0)
    def _():
        for s in range(leaves):
            high[s], low[s] = split(uppers[s][...])

    for k in range(kblocks):
        out_ref[:, k * BLOCK : (k + 1) * BLOCK] = parent_ref[pl.ds(k, BLOCK, stride=kblocks), :]
    for s in range(leaves):
        oks = [rok[(s * capacity + t) * steps + p] for t in range(capacity)]

        @pl.when(sum(oks) > 0)
        def _():
            parts = split(factors[s][...])
            for k in range(kblocks):
                m = cfrom[s * kblocks + k]

                @pl.when(cok[s * kblocks + k] > 0)
                def _():
                    start = pl.multiple_of(m * BLOCK, BLOCK)
                    cut = pl.ds(start, BLOCK)
                    value = -dot_split(parts, (high[s, :, cut], low[s, :, cut]))
                    for t in range(capacity):
                        for n in range(capacity):
                            take = (oks[t] > 0) & (m % capacity == n)
                            block = blocks[s * squares + t * capacity + n][m // capacity]
                            value = value + jnp.where(take, block, 0.0)
                    out_ref[:, k * BLOCK : (k + 1) * BLOCK] += value


def assemble(parent, pieces, factors, uppers, leaves, capacity, kblocks, tables):
    per_row = parent.shape[0] // (BLOCK * kblocks)
    ends = pieces[0].shape[1]
    width = uppers[0].shape[1]

    def piece_spec(n):
        place = n // capacity
        return pl.BlockSpec(
            (None, ends, BLOCK, BLOCK),
            lambda i, rf, *_: (rf[place * per_row + i], 0, 0, 0),
        )

    def factor_spec(s):
        return pl.BlockSpec(
            (BLOCK, PANEL), lambda i, rf, ro, rs, cf, co: (rs[s * per_row + i], 0)
        )

    return pl.pallas_call(
        functools.partial(assemble_kernel, leaves, capacity, kblocks),
        grid_spec=pltpu.PrefetchScalarGridSpec(
            num_scalar_prefetch=5,
            grid=(per_row,),
            in_specs=[pl.BlockSpec((BLOCK * kblocks, BLOCK), lambda i, *_: (i, 0))]
            + [piece_spec(n) for n in range(len(pieces))]
            + [factor_spec(s) for s in range(leaves)]
            + [pl.BlockSpec((PANEL, width), lambda i, *_: (0, 0))] * leaves,
            out_specs=pl.BlockSpec((BLOCK, kblocks * BLOCK), lambda i, *_: (i, 0)),
            scratch_shapes=[pltpu.VMEM((leaves, PANEL, width), jnp.bfloat16)] * 2,
        ),
        out_shape=jax.ShapeDtypeStruct((per_row * BLOCK, kblocks * BLOCK), F32),
        compiler_params=pltpu.CompilerParams(vmem_limit_bytes=48 * 2**20),
        name="assemble",
    )(*tables, parent, *pieces, *factors, *uppers)


def update_kernel(kblocks, lead, place, a_ref, p0_ref, p1_ref, inv_ref, top_ref, out_ref, ih, il, uh, ul):
    p = pl.program_id(0)
    rows = a_ref.shape[0]

    @pl.when(p == 0)
    def _():
        ih[...], il[...] = split(inv_ref[...].T)
        uh[...], ul[...] = split(dot(inv_ref[...], top_ref[...]))

    factor = dot_split(split(p0_ref[...]), (ih[:BLOCK], il[:BLOCK]))
    factor = factor + dot_split(split(p1_ref[...]), (ih[BLOCK:], il[BLOCK:]))
    parts = split(factor)
    line = lax.broadcasted_iota(jnp.int32, (rows, BLOCK), 0) + p * rows
    keep = (place[0] == 0) & (line < lead * BLOCK)
    for k in range(kblocks):
        span = slice(k * BLOCK, (k + 1) * BLOCK)
        mine = a_ref[:, span]
        value = jnp.where(keep, mine, mine - dot_split(parts, (uh[:, span], ul[:, span])))
        if k == 0:
            for block in range(lead):
                piece = factor[:, block * BLOCK : (block + 1) * BLOCK]
                value = jnp.where(place[1] == block, piece, value)
        out_ref[pl.ds(k, rows, stride=kblocks), :] = value


def update(assembled, panel0, panel1, inverse, top, place, kblocks):
    rows, width = assembled.shape
    tall = 2 * PANEL
    return pl.pallas_call(
        functools.partial(update_kernel, kblocks, PANEL // BLOCK),
        grid_spec=pltpu.PrefetchScalarGridSpec(
            num_scalar_prefetch=1,
            grid=(rows // tall,),
            in_specs=[
                pl.BlockSpec((tall, width), lambda i, _: (i, 0)),
                pl.BlockSpec((tall, BLOCK), lambda i, _: (i, 0)),
                pl.BlockSpec((tall, BLOCK), lambda i, _: (i, 0)),
                pl.BlockSpec((PANEL, PANEL), lambda i, _: (0, 0)),
                pl.BlockSpec((PANEL, width), lambda i, _: (0, 0)),
            ],
            out_specs=pl.BlockSpec((tall * kblocks, BLOCK), lambda i, _: (i, 0)),
            scratch_shapes=[pltpu.VMEM((PANEL, PANEL), jnp.bfloat16)] * 2
            + [pltpu.VMEM((PANEL, width), jnp.bfloat16)] * 2,
        ),
        out_shape=jax.ShapeDtypeStruct((rows * kblocks, BLOCK), F32),
        compiler_params=pltpu.CompilerParams(vmem_limit_bytes=40 * 2**20),
        name="update",
    )(place, assembled, panel0, panel1, inverse, top)


def ranks(targets, usable):
    count = targets.shape[-1]
    same = (targets[..., :, None] == targets[..., None, :]) & usable[..., None, :]
    before = jnp.arange(count)[None, :] < jnp.arange(count)[:, None]
    return jnp.sum(same & before, axis=-1)


def per_device(child_front, parent_front, block_map):
    front = child_front[0]
    grid_rows = lax.axis_size("row")
    grid_cols = lax.axis_size("col")
    leaves = lax.axis_size("leaf")
    row_id = lax.axis_index("row")
    col_id = lax.axis_index("col")
    leaf_id = lax.axis_index("leaf")
    blocks = front.shape[0] // BLOCK
    capacity = max(1, blocks // grid_rows)
    parent_rows, kblocks = parent_front.shape[:2]
    per_row = parent_rows // BLOCK
    period = leaves * grid_cols
    lead = PANEL // BLOCK

    padded = jnp.concatenate([jnp.full((leaves, lead), -1, jnp.int32), block_map], axis=1)
    maps = padded.reshape(leaves, grid_rows, blocks)
    usable = maps >= 0
    to_row = jnp.where(usable, maps // per_row, -1)
    to_col = jnp.where(usable, maps % grid_cols, -1)
    row_rank = ranks(to_row, usable)
    col_rank = ranks(to_col, usable)
    positions = jnp.arange(blocks)

    def picks(target, rank, group, count):
        target = target[leaf_id, group]
        rank = rank[leaf_id, group]
        chosen = (target == jnp.arange(count)[:, None, None]) & (
            rank == jnp.arange(capacity)[None, :, None]
        )
        return jnp.sum(jnp.where(chosen, positions, 0), axis=-1).astype(jnp.int32)

    row_ids = picks(to_row, row_rank, row_id, grid_rows)
    col_ids = picks(to_col, col_rank, col_id, grid_cols).reshape(-1)

    row_list = row_ids.reshape(-1)
    sends = pick_blocks(front, row_list, col_ids, capacity)

    corner = spread(spread(front[:PANEL, :PANEL], "row", 1), "col", 1)
    panel = spread(front[:, :PANEL], "col", 1)

    own_map = maps[leaf_id]
    corner_at = []
    for group_id in (row_id, col_id):
        for block in range(lead):
            found = own_map[group_id] == block
            corner_at.append((jnp.sum(jnp.where(found, positions, 0)), jnp.any(found)))
    rows_at, cols_at = corner_at[:lead], corner_at[lead:]

    def cut(x, i, j, wide, ok):
        block = lax.dynamic_slice(x, (i * BLOCK, j * BLOCK), (BLOCK, wide))
        return jnp.where(ok, block, 0.0)

    parent_flat = parent_front.reshape(parent_rows, kblocks, BLOCK)
    device = leaf_id * grid_cols + col_id
    raw = jnp.block(
        [[cut(front, i, j, BLOCK, a & b) for j, b in cols_at] for i, a in rows_at]
    )
    first = parent_flat[:PANEL, 0, :]
    raw = raw + jnp.concatenate(
        [jnp.where((row_id == 0) & (device == block), first, 0.0) for block in range(lead)], axis=1
    )
    touched = jnp.concatenate(
        [cut(front, i, 0, PANEL, a & (col_id == 0)) for i, a in rows_at], axis=0
    )
    raw, touched = lax.psum((raw, touched), ("row", "col"))

    order = (leaf_id - jnp.arange(leaves)) % leaves
    maps_here = maps[order]
    row_rank_here = row_rank[order]
    col_rank_here = col_rank[order]
    group = jnp.arange(grid_rows)[None, None, :, None]
    hit = maps_here[:, None] == (row_id * per_row + jnp.arange(per_row))[None, :, None, None]
    in_chunk = row_rank_here[:, None, None] == jnp.arange(capacity)[None, :, None, None, None]
    hit_chunk = hit[:, None] & in_chunk
    rfrom = jnp.sum(jnp.where(hit_chunk, group[:, None], 0), axis=(-1, -2))
    rok = jnp.sum(hit_chunk, axis=(-1, -2))
    slot = group * capacity + row_rank_here[:, None]
    rslot = jnp.sum(jnp.where(hit, slot, 0), axis=(-1, -2))
    owned = jnp.arange(kblocks) * period + device
    hit = maps_here[:, None] == owned[None, :, None, None]
    slot = group * capacity + col_rank_here[:, None]
    cfrom = jnp.sum(jnp.where(hit, slot, 0), axis=(-1, -2))
    cok = jnp.sum(hit, axis=(-1, -2))
    tables = [x.reshape(-1).astype(jnp.int32) for x in (rfrom, rok, rslot, cfrom, cok)]

    def exchange(x):
        return lax.all_to_all(x, ("row", "col"), split_axis=0, concat_axis=0, tiled=True)

    def leaf_copies(x):
        pairs = lambda shift: [(i, (i + shift) % leaves) for i in range(leaves)]
        return [x] + [lax.ppermute(x, "leaf", pairs(shift)) for shift in range(1, leaves)]

    by_block = panel.reshape(blocks, BLOCK, PANEL)
    picked = jnp.take(by_block, row_list, axis=0).reshape(grid_rows, capacity, BLOCK, PANEL)
    mine_cols = picks(to_col, col_rank, row_id, grid_cols)[col_id]
    for_cols = jnp.take(by_block, mine_cols, axis=0)
    packed = jnp.concatenate(
        [picked, jnp.broadcast_to(for_cols[None], (grid_rows, *for_cols.shape))], axis=1
    )

    inverse = lower_inverse(corner[:, :BLOCK], corner[:, BLOCK:])
    factor = dot(panel, inverse, ((1,), (1,)))
    half = dot(touched, inverse, ((1,), (1,)))
    corner_parent = lax.psum(raw - dot(half, half, ((1,), (1,))), "leaf")
    inverse_parent = lower_inverse(corner_parent[:, :BLOCK], corner_parent[:, BLOCK:])

    pieces = [[] for _ in range(leaves)]
    for out in sends:
        got = exchange(out.reshape(grid_rows * grid_cols, BLOCK, BLOCK))
        for shift, moved in enumerate(leaf_copies(got)):
            pieces[shift].append(moved.reshape(grid_rows, grid_cols, BLOCK, BLOCK))
    pieces = [x for part in pieces for x in part]
    got = lax.all_to_all(packed, "row", split_axis=0, concat_axis=0, tiled=True)
    factors, uppers = [], []
    for rows, inv in zip(leaf_copies(got), leaf_copies(inverse)):
        slots = grid_rows * capacity
        factors.append(dot(rows[:, :capacity].reshape(slots * BLOCK, PANEL), inv, ((1,), (1,))))
        uppers.append(dot(inv, rows[:, capacity:].reshape(slots * BLOCK, PANEL), ((1,), (1,))))
    assembled = assemble(
        parent_front.reshape(parent_rows * kblocks, BLOCK),
        pieces, factors, uppers, leaves, capacity, kblocks, tables,
    )

    panel = assembled[:, :BLOCK]
    middle = parent_rows // 2
    upper_half = spread(spread(panel[:middle], "col", 2), "leaf", 1)
    lower_half = spread(spread(panel[middle:], "leaf", 1), "col", 2)
    top = spread(assembled[:PANEL], "row", 1)
    panel0, panel1 = swap_pairs(jnp.concatenate([upper_half, lower_half], axis=0))
    place = jnp.stack([row_id, device]).astype(jnp.int32)
    result = update(assembled, panel0, panel1, inverse_parent, top, place, kblocks)
    return factor[None], result.reshape(parent_front.shape)


def solution(mesh):
    placed = (P("leaf", "row", "col"), P("row", None, ("leaf", "col"), None), P())
    return jax.shard_map(
        per_device,
        mesh=mesh,
        in_specs=placed,
        out_specs=(P("leaf", "row", None), P("row", None, ("leaf", "col"), None)),
        check_vma=False,
    )
```

```python
import functools

import jax
import jax.numpy as jnp
from jax import lax
from jax.experimental import pallas as pl
from jax.experimental.pallas import tpu as pltpu
from jax.sharding import PartitionSpec as P

PANEL = 256
BLOCK = 128
STEP = 64
HIGH = lax.Precision.HIGHEST
F32 = jnp.float32


def dot(left, right, dims=((1,), (0,))):
    return lax.dot_general(left, right, (dims, ((), ())), precision=HIGH, preferred_element_type=F32)


def split(x):
    high = x.astype(jnp.bfloat16)
    return high, (x - high.astype(F32)).astype(jnp.bfloat16)


def dot_split(left, right):
    one = lambda a, b: jnp.dot(a, b, preferred_element_type=F32)
    return one(left[0], right[0]) + (one(left[0], right[1]) + one(left[1], right[0]))


def spread(x, axis, unit):
    n = lax.axis_size(axis)
    here = lax.axis_index(axis)
    stride = n // 2
    while stride >= unit:
        pairs = [
            (i + e, i + stride + e) for i in range(0, n, 2 * stride) for e in range(unit)
        ]
        got = lax.ppermute(x, axis, pairs)
        inside = here % (2 * stride)
        x = jnp.where((inside >= stride) & (inside < stride + unit), got, x)
        stride //= 2
    return x


def swap_pairs(x):
    n = lax.axis_size("col")
    here = lax.axis_index("col")
    got = lax.ppermute(x, "col", [(i, i ^ 1) for i in range(n)])
    even = here % 2 == 0
    return jnp.where(even, x, got), jnp.where(even, got, x)


def invert_kernel(left_ref, right_ref, out_ref, work):
    work[:, 0:BLOCK] = left_ref[...]
    work[:, BLOCK:PANEL] = right_ref[...]
    rows = lax.broadcasted_iota(jnp.int32, (PANEL, PANEL), 0)
    cols = lax.broadcasted_iota(jnp.int32, (PANEL, PANEL), 1)
    work[:, PANEL:] = (rows == cols).astype(F32)
    groups = STEP // 8
    sub = lax.broadcasted_iota(jnp.int32, (8, 1), 0)
    lane8 = lax.broadcasted_iota(jnp.int32, (8, BLOCK), 1)
    sub8 = lax.broadcasted_iota(jnp.int32, (8, BLOCK), 0)
    for s in range(PANEL // STEP):
        top = s * STEP
        tile = top // BLOCK * BLOCK
        off = top - tile
        d = [work[top + 8 * g : top + 8 * g + 8, tile : tile + BLOCK] for g in range(groups)]
        w = [(lane8 == sub8 + 8 * g).astype(F32) for g in range(groups)]
        for j in range(STEP):
            g0 = j // 8
            r = j % 8
            drow = d[g0][r : r + 1, :]
            wrow = w[g0][r : r + 1, :]
            inv = 1.0 / drow[:, off + j : off + j + 1]
            drow = drow * inv
            wrow = wrow * inv
            for g in range(g0, groups):
                f = d[g][:, off + j : off + j + 1]
                if g == g0:
                    if r == 7:
                        continue
                    f = jnp.where(sub > r, f, 0.0)
                d[g] = d[g] - f * drow
                w[g] = w[g] - f * wrow
        scaled = []
        for g in range(groups):
            diag = jnp.sum(jnp.where(lane8 == sub8 + (off + 8 * g), d[g], 0.0), axis=1, keepdims=True)
            scaled.append(w[g] * lax.rsqrt(diag))
        wide = jnp.concatenate(scaled, axis=0)[:, :STEP]
        strip = dot(wide, work[top : top + STEP, :])
        work[top : top + STEP, :] = strip
        if top + STEP < PANEL:
            change = dot(strip[:, :PANEL], strip, ((0,), (0,)))
            work[top + STEP :, :] = work[top + STEP :, :] - change[top + STEP :, :]
    out_ref[...] = work[:, PANEL:]


def lower_inverse(left, right):
    return pl.pallas_call(
        invert_kernel,
        out_shape=jax.ShapeDtypeStruct((PANEL, PANEL), F32),
        scratch_shapes=[pltpu.VMEM((PANEL, 2 * PANEL), F32)],
        cost_estimate=pl.CostEstimate(flops=10**10, bytes_accessed=10**8, transcendentals=0),
        name="invert",
    )(left, right)


def schur_kernel(slots, row_ids, col_ids, a_ref, f_ref, u_ref, out_ref, strip):
    strip[...] = a_ref[...] - dot(f_ref[...], u_ref[...])
    for m in range(slots):
        start = pl.multiple_of(col_ids[m] * BLOCK, BLOCK)
        out_ref[m] = strip[:, pl.ds(start, BLOCK)]


def schur_pick(front, factor, upper, row_ids, col_ids):
    dests, slots = row_ids.shape[0], col_ids.shape[0]
    width = front.shape[1]
    return pl.pallas_call(
        functools.partial(schur_kernel, slots),
        grid_spec=pltpu.PrefetchScalarGridSpec(
            num_scalar_prefetch=2,
            grid=(dests,),
            in_specs=[
                pl.BlockSpec((BLOCK, width), lambda i, r, c: (r[i], 0)),
                pl.BlockSpec((BLOCK, PANEL), lambda i, r, c: (r[i], 0)),
                pl.BlockSpec((PANEL, width), lambda i, r, c: (0, 0)),
            ],
            out_specs=pl.BlockSpec((None, slots, BLOCK, BLOCK), lambda i, r, c: (i, 0, 0, 0)),
            scratch_shapes=[pltpu.VMEM((BLOCK, width), F32)],
        ),
        out_shape=jax.ShapeDtypeStruct((dests, slots, BLOCK, BLOCK), F32),
        cost_estimate=pl.CostEstimate(
            flops=12 * dests * BLOCK * PANEL * width,
            bytes_accessed=8 * dests * BLOCK * width,
            transcendentals=0,
        ),
        name="schur",
    )(row_ids, col_ids, front, factor, upper)


def assemble_kernel(leaves, capacity, kblocks, rfrom, rok, cfrom, cok, parent_ref, *refs):
    out_ref = refs[-1]
    p = pl.program_id(0)
    for k in range(kblocks):
        total = parent_ref[pl.ds(k, BLOCK, stride=kblocks), :]
        for s in range(leaves):
            m = cfrom[s * kblocks + k]
            for t in range(capacity):
                ok = rok[(s * capacity + t) * pl.num_programs(0) + p] * cok[s * kblocks + k]
                total = total + jnp.where(ok > 0, refs[s * capacity + t][m], 0.0)
        out_ref[:, k * BLOCK : (k + 1) * BLOCK] = total


def assemble(parent, pieces, leaves, capacity, kblocks, rfrom, rok, cfrom, cok):
    per_row = parent.shape[0] // (BLOCK * kblocks)
    slots = pieces[0].shape[1]

    def piece_spec(n):
        return pl.BlockSpec(
            (None, slots, BLOCK, BLOCK), lambda i, rf, ro, cf, co: (rf[n * per_row + i], 0, 0, 0)
        )

    return pl.pallas_call(
        functools.partial(assemble_kernel, leaves, capacity, kblocks),
        grid_spec=pltpu.PrefetchScalarGridSpec(
            num_scalar_prefetch=4,
            grid=(per_row,),
            in_specs=[pl.BlockSpec((BLOCK * kblocks, BLOCK), lambda i, *_: (i, 0))]
            + [piece_spec(n) for n in range(len(pieces))],
            out_specs=pl.BlockSpec((BLOCK, kblocks * BLOCK), lambda i, *_: (i, 0)),
        ),
        out_shape=jax.ShapeDtypeStruct((per_row * BLOCK, kblocks * BLOCK), F32),
        compiler_params=pltpu.CompilerParams(vmem_limit_bytes=40 * 2**20),
        name="assemble",
    )(rfrom, rok, cfrom, cok, parent, *pieces)


def update_kernel(kblocks, lead, place, a_ref, p0_ref, p1_ref, inv_ref, top_ref, out_ref, ih, il, uh, ul):
    p = pl.program_id(0)
    rows = a_ref.shape[0]

    @pl.when(p == 0)
    def _():
        ih[...], il[...] = split(inv_ref[...].T)
        uh[...], ul[...] = split(dot(inv_ref[...], top_ref[...]))

    factor = dot_split(split(p0_ref[...]), (ih[:BLOCK], il[:BLOCK]))
    factor = factor + dot_split(split(p1_ref[...]), (ih[BLOCK:], il[BLOCK:]))
    parts = split(factor)
    line = lax.broadcasted_iota(jnp.int32, (rows, BLOCK), 0) + p * rows
    keep = (place[0] == 0) & (line < lead * BLOCK)
    for k in range(kblocks):
        span = slice(k * BLOCK, (k + 1) * BLOCK)
        mine = a_ref[:, span]
        value = jnp.where(keep, mine, mine - dot_split(parts, (uh[:, span], ul[:, span])))
        if k == 0:
            for block in range(lead):
                piece = factor[:, block * BLOCK : (block + 1) * BLOCK]
                value = jnp.where(place[1] == block, piece, value)
        out_ref[pl.ds(k, rows, stride=kblocks), :] = value


def update(assembled, panel0, panel1, inverse, top, place, kblocks):
    rows, width = assembled.shape
    tall = 2 * PANEL
    return pl.pallas_call(
        functools.partial(update_kernel, kblocks, PANEL // BLOCK),
        grid_spec=pltpu.PrefetchScalarGridSpec(
            num_scalar_prefetch=1,
            grid=(rows // tall,),
            in_specs=[
                pl.BlockSpec((tall, width), lambda i, _: (i, 0)),
                pl.BlockSpec((tall, BLOCK), lambda i, _: (i, 0)),
                pl.BlockSpec((tall, BLOCK), lambda i, _: (i, 0)),
                pl.BlockSpec((PANEL, PANEL), lambda i, _: (0, 0)),
                pl.BlockSpec((PANEL, width), lambda i, _: (0, 0)),
            ],
            out_specs=pl.BlockSpec((tall * kblocks, BLOCK), lambda i, _: (i, 0)),
            scratch_shapes=[pltpu.VMEM((PANEL, PANEL), jnp.bfloat16)] * 2
            + [pltpu.VMEM((PANEL, width), jnp.bfloat16)] * 2,
        ),
        out_shape=jax.ShapeDtypeStruct((rows * kblocks, BLOCK), F32),
        compiler_params=pltpu.CompilerParams(vmem_limit_bytes=40 * 2**20),
        name="update",
    )(place, assembled, panel0, panel1, inverse, top)


def ranks(targets, usable):
    count = targets.shape[-1]
    same = (targets[..., :, None] == targets[..., None, :]) & usable[..., None, :]
    before = jnp.arange(count)[None, :] < jnp.arange(count)[:, None]
    return jnp.sum(same & before, axis=-1)


def per_device(child_front, parent_front, block_map):
    front = child_front[0]
    grid_rows = lax.axis_size("row")
    grid_cols = lax.axis_size("col")
    leaves = lax.axis_size("leaf")
    row_id = lax.axis_index("row")
    col_id = lax.axis_index("col")
    leaf_id = lax.axis_index("leaf")
    blocks = front.shape[0] // BLOCK
    capacity = max(1, blocks // grid_rows)
    parent_rows, kblocks = parent_front.shape[:2]
    per_row = parent_rows // BLOCK
    period = leaves * grid_cols
    lead = PANEL // BLOCK

    corner = spread(spread(front[:PANEL, :PANEL], "row", 1), "col", 1)
    top_rows = spread(front[:PANEL, :], "row", 1)
    panel_rows = spread(front[:, :PANEL], "col", 1)
    inverse = lower_inverse(corner[:, :BLOCK], corner[:, BLOCK:])

    padded = jnp.concatenate([jnp.full((leaves, lead), -1, jnp.int32), block_map], axis=1)
    maps = padded.reshape(leaves, grid_rows, blocks)
    usable = maps >= 0
    to_row = jnp.where(usable, maps // per_row, -1)
    to_col = jnp.where(usable, maps % grid_cols, -1)
    row_rank = ranks(to_row, usable)
    col_rank = ranks(to_col, usable)
    positions = jnp.arange(blocks)

    def picks(target, rank, group, count):
        target = target[leaf_id, group]
        rank = rank[leaf_id, group]
        chosen = (target == jnp.arange(count)[:, None, None]) & (
            rank == jnp.arange(capacity)[None, :, None]
        )
        return jnp.sum(jnp.where(chosen, positions, 0), axis=-1).astype(jnp.int32)

    row_ids = picks(to_row, row_rank, row_id, grid_rows)
    col_ids = picks(to_col, col_rank, col_id, grid_cols).reshape(-1)

    order = (leaf_id - jnp.arange(leaves)) % leaves
    maps_here = maps[order]
    row_rank_here = row_rank[order]
    col_rank_here = col_rank[order]
    group = jnp.arange(grid_rows)[None, None, :, None]
    hit = maps_here[:, None] == (row_id * per_row + jnp.arange(per_row))[None, :, None, None]
    in_chunk = row_rank_here[:, None, None] == jnp.arange(capacity)[None, :, None, None, None]
    hit_chunk = hit[:, None] & in_chunk
    rfrom = jnp.sum(jnp.where(hit_chunk, group[:, None], 0), axis=(-1, -2))
    rok = jnp.sum(hit_chunk, axis=(-1, -2))
    owned = jnp.arange(kblocks) * period + leaf_id * grid_cols + col_id
    hit = maps_here[:, None] == owned[None, :, None, None]
    slot = group * capacity + col_rank_here[:, None]
    cfrom = jnp.sum(jnp.where(hit, slot, 0), axis=(-1, -2))
    cok = jnp.sum(hit, axis=(-1, -2))
    rfrom, rok, cfrom, cok = [x.reshape(-1).astype(jnp.int32) for x in (rfrom, rok, cfrom, cok)]

    factor = dot(panel_rows, inverse, ((1,), (1,)))
    upper = dot(inverse, top_rows)
    own = []
    for t in range(capacity):
        out = schur_pick(front, factor, upper, row_ids[:, t], col_ids)
        out = out.reshape(grid_rows * grid_cols, capacity, BLOCK, BLOCK)
        got = lax.all_to_all(out, ("row", "col"), split_axis=0, concat_axis=0, tiled=True)
        own.append(got)
    own_map = maps[leaf_id]
    device = leaf_id * grid_cols + col_id

    def place_of(group_id, block):
        found = own_map[group_id] == block
        return jnp.sum(jnp.where(found, positions, 0)), jnp.any(found)

    rows_at = [place_of(row_id, block) for block in range(lead)]
    cols_at = [place_of(col_id, block) for block in range(lead)]

    def cut(x, i, j, shape, ok):
        return jnp.where(ok, lax.dynamic_slice(x, (i * BLOCK, j * BLOCK), shape), 0.0)

    square = (BLOCK, BLOCK)
    share = jnp.block([[cut(front, i, j, square, a & b) for j, b in cols_at] for i, a in rows_at])
    left = jnp.concatenate([cut(factor, i, 0, (BLOCK, PANEL), a) for i, a in rows_at], axis=0)
    right = jnp.concatenate([cut(upper, 0, j, (PANEL, BLOCK), b) for j, b in cols_at], axis=1)
    first = parent_front[:PANEL, 0, 0, :]
    given = jnp.concatenate(
        [jnp.where((row_id == 0) & (device == block), first, 0.0) for block in range(lead)], axis=1
    )
    corner_parent = lax.psum(given + (share - dot(left, right)), ("leaf", "row", "col"))
    corner_parent, own[-1] = lax.optimization_barrier((corner_parent, own[-1]))
    inverse_parent = lower_inverse(corner_parent[:, :BLOCK], corner_parent[:, BLOCK:])

    pieces = [[] for _ in range(leaves)]
    for got in own:
        for shift in range(leaves):
            moved = got
            if shift:
                pairs = [(i, (i + shift) % leaves) for i in range(leaves)]
                moved = lax.ppermute(got, "leaf", pairs)
            pieces[shift].append(
                moved.reshape(grid_rows, grid_cols * capacity, BLOCK, BLOCK)
            )
    pieces = [x for part in pieces for x in part]
    inverse_parent, rok = lax.optimization_barrier((inverse_parent, rok))
    assembled = assemble(
        parent_front.reshape(parent_rows * kblocks, BLOCK),
        pieces, leaves, capacity, kblocks, rfrom, rok, cfrom, cok,
    )

    panel = assembled[:, :BLOCK]
    middle = parent_rows // 2
    upper_half = spread(spread(panel[:middle], "col", 2), "leaf", 1)
    lower_half = spread(spread(panel[middle:], "leaf", 1), "col", 2)
    top = spread(assembled[:PANEL], "row", 1)
    panel0, panel1 = swap_pairs(jnp.concatenate([upper_half, lower_half], axis=0))
    place = jnp.stack([row_id, device]).astype(jnp.int32)
    result = update(assembled, panel0, panel1, inverse_parent, top, place, kblocks)
    return factor[None], result.reshape(parent_front.shape)


def solution(mesh):
    placed = (P("leaf", "row", "col"), P("row", None, ("leaf", "col"), None), P())
    return jax.shard_map(
        per_device,
        mesh=mesh,
        in_specs=placed,
        out_specs=(P("leaf", "row", None), P("row", None, ("leaf", "col"), None)),
        check_vma=False,
    )
```

```python
import functools

import jax
import jax.numpy as jnp
from jax import lax
from jax.experimental import pallas as pl
from jax.experimental.pallas import tpu as pltpu
from jax.sharding import PartitionSpec as P

PANEL = 256
BLOCK = 128
STEP = 64
HIGH = lax.Precision.HIGHEST
F32 = jnp.float32


def dot(left, right, dims=((1,), (0,))):
    return lax.dot_general(left, right, (dims, ((), ())), precision=HIGH, preferred_element_type=F32)


def split(x):
    high = x.astype(jnp.bfloat16)
    return high, (x - high.astype(F32)).astype(jnp.bfloat16)


def dot_split(left, right):
    one = lambda a, b: jnp.dot(a, b, preferred_element_type=F32)
    return one(left[0], right[0]) + (one(left[0], right[1]) + one(left[1], right[0]))


def spread(x, axis, unit):
    n = lax.axis_size(axis)
    here = lax.axis_index(axis)
    stride = n // 2
    while stride >= unit:
        pairs = [
            (i + e, i + stride + e) for i in range(0, n, 2 * stride) for e in range(unit)
        ]
        got = lax.ppermute(x, axis, pairs)
        inside = here % (2 * stride)
        x = jnp.where((inside >= stride) & (inside < stride + unit), got, x)
        stride //= 2
    return x


def swap_pairs(x):
    n = lax.axis_size("col")
    here = lax.axis_index("col")
    got = lax.ppermute(x, "col", [(i, i ^ 1) for i in range(n)])
    even = here % 2 == 0
    return jnp.where(even, x, got), jnp.where(even, got, x)


def invert_kernel(left_ref, right_ref, out_ref, work):
    work[:, 0:BLOCK] = left_ref[...]
    work[:, BLOCK:PANEL] = right_ref[...]
    rows = lax.broadcasted_iota(jnp.int32, (PANEL, PANEL), 0)
    cols = lax.broadcasted_iota(jnp.int32, (PANEL, PANEL), 1)
    work[:, PANEL:] = (rows == cols).astype(F32)
    groups = STEP // 8
    sub = lax.broadcasted_iota(jnp.int32, (8, 1), 0)
    lane8 = lax.broadcasted_iota(jnp.int32, (8, BLOCK), 1)
    sub8 = lax.broadcasted_iota(jnp.int32, (8, BLOCK), 0)
    for s in range(PANEL // STEP):
        top = s * STEP
        tile = top // BLOCK * BLOCK
        off = top - tile
        d = [work[top + 8 * g : top + 8 * g + 8, tile : tile + BLOCK] for g in range(groups)]
        w = [(lane8 == sub8 + 8 * g).astype(F32) for g in range(groups)]
        for j in range(STEP):
            g0 = j // 8
            r = j % 8
            drow = d[g0][r : r + 1, :]
            wrow = w[g0][r : r + 1, :]
            inv = 1.0 / drow[:, off + j : off + j + 1]
            drow = drow * inv
            wrow = wrow * inv
            for g in range(g0, groups):
                f = d[g][:, off + j : off + j + 1]
                if g == g0:
                    if r == 7:
                        continue
                    f = jnp.where(sub > r, f, 0.0)
                d[g] = d[g] - f * drow
                w[g] = w[g] - f * wrow
        scaled = []
        for g in range(groups):
            diag = jnp.sum(jnp.where(lane8 == sub8 + (off + 8 * g), d[g], 0.0), axis=1, keepdims=True)
            scaled.append(w[g] * lax.rsqrt(diag))
        wide = jnp.concatenate(scaled, axis=0)[:, :STEP]
        strip = dot(wide, work[top : top + STEP, :])
        work[top : top + STEP, :] = strip
        if top + STEP < PANEL:
            change = dot(strip[:, :PANEL], strip, ((0,), (0,)))
            work[top + STEP :, :] = work[top + STEP :, :] - change[top + STEP :, :]
    out_ref[...] = work[:, PANEL:]


def lower_inverse(left, right):
    return pl.pallas_call(
        invert_kernel,
        out_shape=jax.ShapeDtypeStruct((PANEL, PANEL), F32),
        scratch_shapes=[pltpu.VMEM((PANEL, 2 * PANEL), F32)],
        cost_estimate=pl.CostEstimate(flops=10**10, bytes_accessed=10**8, transcendentals=0),
        name="invert",
    )(left, right)


def schur_kernel(slots, row_ids, col_ids, a_ref, f_ref, u_ref, out_ref, strip):
    strip[...] = a_ref[...] - dot(f_ref[...], u_ref[...])
    for m in range(slots):
        start = pl.multiple_of(col_ids[m] * BLOCK, BLOCK)
        out_ref[m] = strip[:, pl.ds(start, BLOCK)]


def schur_pick(front, factor, upper, row_ids, col_ids):
    dests, slots = row_ids.shape[0], col_ids.shape[0]
    width = front.shape[1]
    return pl.pallas_call(
        functools.partial(schur_kernel, slots),
        grid_spec=pltpu.PrefetchScalarGridSpec(
            num_scalar_prefetch=2,
            grid=(dests,),
            in_specs=[
                pl.BlockSpec((BLOCK, width), lambda i, r, c: (r[i], 0)),
                pl.BlockSpec((BLOCK, PANEL), lambda i, r, c: (r[i], 0)),
                pl.BlockSpec((PANEL, width), lambda i, r, c: (0, 0)),
            ],
            out_specs=pl.BlockSpec((None, slots, BLOCK, BLOCK), lambda i, r, c: (i, 0, 0, 0)),
            scratch_shapes=[pltpu.VMEM((BLOCK, width), F32)],
        ),
        out_shape=jax.ShapeDtypeStruct((dests, slots, BLOCK, BLOCK), F32),
        cost_estimate=pl.CostEstimate(
            flops=12 * dests * BLOCK * PANEL * width,
            bytes_accessed=8 * dests * BLOCK * width,
            transcendentals=0,
        ),
        name="schur",
    )(row_ids, col_ids, front, factor, upper)


def assemble_kernel(leaves, capacity, kblocks, rfrom, rok, cfrom, cok, parent_ref, *refs):
    out_ref = refs[-1]
    p = pl.program_id(0)
    for k in range(kblocks):
        total = parent_ref[pl.ds(k, BLOCK, stride=kblocks), :]
        for s in range(leaves):
            m = cfrom[s * kblocks + k]
            for t in range(capacity):
                ok = rok[(s * capacity + t) * pl.num_programs(0) + p] * cok[s * kblocks + k]
                total = total + jnp.where(ok > 0, refs[s * capacity + t][m], 0.0)
        out_ref[:, k * BLOCK : (k + 1) * BLOCK] = total


def assemble(parent, pieces, leaves, capacity, kblocks, rfrom, rok, cfrom, cok):
    per_row = parent.shape[0] // (BLOCK * kblocks)
    slots = pieces[0].shape[1]

    def piece_spec(n):
        return pl.BlockSpec(
            (None, slots, BLOCK, BLOCK), lambda i, rf, ro, cf, co: (rf[n * per_row + i], 0, 0, 0)
        )

    return pl.pallas_call(
        functools.partial(assemble_kernel, leaves, capacity, kblocks),
        grid_spec=pltpu.PrefetchScalarGridSpec(
            num_scalar_prefetch=4,
            grid=(per_row,),
            in_specs=[pl.BlockSpec((BLOCK * kblocks, BLOCK), lambda i, *_: (i, 0))]
            + [piece_spec(n) for n in range(len(pieces))],
            out_specs=pl.BlockSpec((BLOCK, kblocks * BLOCK), lambda i, *_: (i, 0)),
        ),
        out_shape=jax.ShapeDtypeStruct((per_row * BLOCK, kblocks * BLOCK), F32),
        compiler_params=pltpu.CompilerParams(vmem_limit_bytes=40 * 2**20),
        name="assemble",
    )(rfrom, rok, cfrom, cok, parent, *pieces)


def update_kernel(kblocks, lead, place, a_ref, p0_ref, p1_ref, inv_ref, top_ref, out_ref, ih, il, uh, ul):
    p = pl.program_id(0)
    rows = a_ref.shape[0]

    @pl.when(p == 0)
    def _():
        ih[...], il[...] = split(inv_ref[...].T)
        uh[...], ul[...] = split(dot(inv_ref[...], top_ref[...]))

    factor = dot_split(split(p0_ref[...]), (ih[:BLOCK], il[:BLOCK]))
    factor = factor + dot_split(split(p1_ref[...]), (ih[BLOCK:], il[BLOCK:]))
    parts = split(factor)
    line = lax.broadcasted_iota(jnp.int32, (rows, BLOCK), 0) + p * rows
    keep = (place[0] == 0) & (line < lead * BLOCK)
    for k in range(kblocks):
        span = slice(k * BLOCK, (k + 1) * BLOCK)
        mine = a_ref[:, span]
        value = jnp.where(keep, mine, mine - dot_split(parts, (uh[:, span], ul[:, span])))
        if k == 0:
            for block in range(lead):
                piece = factor[:, block * BLOCK : (block + 1) * BLOCK]
                value = jnp.where(place[1] == block, piece, value)
        out_ref[pl.ds(k, rows, stride=kblocks), :] = value


def update(assembled, panel0, panel1, inverse, top, place, kblocks):
    rows, width = assembled.shape
    tall = 2 * PANEL
    return pl.pallas_call(
        functools.partial(update_kernel, kblocks, PANEL // BLOCK),
        grid_spec=pltpu.PrefetchScalarGridSpec(
            num_scalar_prefetch=1,
            grid=(rows // tall,),
            in_specs=[
                pl.BlockSpec((tall, width), lambda i, _: (i, 0)),
                pl.BlockSpec((tall, BLOCK), lambda i, _: (i, 0)),
                pl.BlockSpec((tall, BLOCK), lambda i, _: (i, 0)),
                pl.BlockSpec((PANEL, PANEL), lambda i, _: (0, 0)),
                pl.BlockSpec((PANEL, width), lambda i, _: (0, 0)),
            ],
            out_specs=pl.BlockSpec((tall * kblocks, BLOCK), lambda i, _: (i, 0)),
            scratch_shapes=[pltpu.VMEM((PANEL, PANEL), jnp.bfloat16)] * 2
            + [pltpu.VMEM((PANEL, width), jnp.bfloat16)] * 2,
        ),
        out_shape=jax.ShapeDtypeStruct((rows * kblocks, BLOCK), F32),
        compiler_params=pltpu.CompilerParams(vmem_limit_bytes=40 * 2**20),
        name="update",
    )(place, assembled, panel0, panel1, inverse, top)


def ranks(targets, usable):
    count = targets.shape[-1]
    same = (targets[..., :, None] == targets[..., None, :]) & usable[..., None, :]
    before = jnp.arange(count)[None, :] < jnp.arange(count)[:, None]
    return jnp.sum(same & before, axis=-1)


def per_device(child_front, parent_front, block_map):
    front = child_front[0]
    grid_rows = lax.axis_size("row")
    grid_cols = lax.axis_size("col")
    leaves = lax.axis_size("leaf")
    row_id = lax.axis_index("row")
    col_id = lax.axis_index("col")
    leaf_id = lax.axis_index("leaf")
    blocks = front.shape[0] // BLOCK
    capacity = max(1, blocks // grid_rows)
    parent_rows, kblocks = parent_front.shape[:2]
    per_row = parent_rows // BLOCK
    period = leaves * grid_cols
    lead = PANEL // BLOCK

    corner = spread(spread(front[:PANEL, :PANEL], "row", 1), "col", 1)
    corner, panel_rows, top_rows = lax.optimization_barrier(
        (corner, front[:, :PANEL], front[:PANEL, :])
    )
    panel_rows = spread(panel_rows, "col", 1)
    top_rows = spread(top_rows, "row", 1)
    inverse = lower_inverse(corner[:, :BLOCK], corner[:, BLOCK:])

    padded = jnp.concatenate([jnp.full((leaves, lead), -1, jnp.int32), block_map], axis=1)
    maps = padded.reshape(leaves, grid_rows, blocks)
    usable = maps >= 0
    to_row = jnp.where(usable, maps // per_row, -1)
    to_col = jnp.where(usable, maps % grid_cols, -1)
    row_rank = ranks(to_row, usable)
    col_rank = ranks(to_col, usable)
    positions = jnp.arange(blocks)

    def picks(target, rank, group, count):
        target = target[leaf_id, group]
        rank = rank[leaf_id, group]
        chosen = (target == jnp.arange(count)[:, None, None]) & (
            rank == jnp.arange(capacity)[None, :, None]
        )
        return jnp.sum(jnp.where(chosen, positions, 0), axis=-1).astype(jnp.int32)

    row_ids = picks(to_row, row_rank, row_id, grid_rows)
    col_ids = picks(to_col, col_rank, col_id, grid_cols).reshape(-1)

    order = (leaf_id - jnp.arange(leaves)) % leaves
    maps_here = maps[order]
    row_rank_here = row_rank[order]
    col_rank_here = col_rank[order]
    group = jnp.arange(grid_rows)[None, None, :, None]
    hit = maps_here[:, None] == (row_id * per_row + jnp.arange(per_row))[None, :, None, None]
    in_chunk = row_rank_here[:, None, None] == jnp.arange(capacity)[None, :, None, None, None]
    hit_chunk = hit[:, None] & in_chunk
    rfrom = jnp.sum(jnp.where(hit_chunk, group[:, None], 0), axis=(-1, -2))
    rok = jnp.sum(hit_chunk, axis=(-1, -2))
    owned = jnp.arange(kblocks) * period + leaf_id * grid_cols + col_id
    hit = maps_here[:, None] == owned[None, :, None, None]
    slot = group * capacity + col_rank_here[:, None]
    cfrom = jnp.sum(jnp.where(hit, slot, 0), axis=(-1, -2))
    cok = jnp.sum(hit, axis=(-1, -2))
    rfrom, rok, cfrom, cok = [x.reshape(-1).astype(jnp.int32) for x in (rfrom, rok, cfrom, cok)]

    factor = dot(panel_rows, inverse, ((1,), (1,)))
    upper = dot(inverse, top_rows)
    own = []
    for t in range(capacity):
        out = schur_pick(front, factor, upper, row_ids[:, t], col_ids)
        out = out.reshape(grid_rows * grid_cols, capacity, BLOCK, BLOCK)
        got = lax.all_to_all(out, ("row", "col"), split_axis=0, concat_axis=0, tiled=True)
        own.append(got)
    pieces = [[] for _ in range(leaves)]
    for got in own:
        for shift in range(leaves):
            moved = got
            if shift:
                pairs = [(i, (i + shift) % leaves) for i in range(leaves)]
                moved = lax.ppermute(got, "leaf", pairs)
            pieces[shift].append(
                moved.reshape(grid_rows, grid_cols * capacity, BLOCK, BLOCK)
            )
    pieces = [x for part in pieces for x in part]
    assembled = assemble(
        parent_front.reshape(parent_rows * kblocks, BLOCK),
        pieces, leaves, capacity, kblocks, rfrom, rok, cfrom, cok,
    )

    piece = spread(spread(assembled[:PANEL, :BLOCK], "col", 2), "leaf", 1)
    piece, panel = lax.optimization_barrier((piece, assembled[:, :BLOCK]))
    middle = parent_rows // 2
    upper_half = spread(spread(panel[:middle], "col", 2), "leaf", 1)
    lower_half = spread(spread(panel[middle:], "leaf", 1), "col", 2)
    panel0, panel1 = swap_pairs(jnp.concatenate([upper_half, lower_half], axis=0))
    corner0, corner1 = swap_pairs(spread(piece, "row", 1))
    corner0, corner1, top = lax.optimization_barrier((corner0, corner1, assembled[:PANEL]))
    top = spread(top, "row", 1)
    inverse_parent = lower_inverse(corner0, corner1)
    place = jnp.stack([row_id, leaf_id * grid_cols + col_id]).astype(jnp.int32)
    result = update(assembled, panel0, panel1, inverse_parent, top, place, kblocks)
    return factor[None], result.reshape(parent_front.shape)


def solution(mesh):
    placed = (P("leaf", "row", "col"), P("row", None, ("leaf", "col"), None), P())
    return jax.shard_map(
        per_device,
        mesh=mesh,
        in_specs=placed,
        out_specs=(P("leaf", "row", None), P("row", None, ("leaf", "col"), None)),
        check_vma=False,
    )
```
